32 devices in a mesh: stream: 2 (over y), ta: 4 (over x, core), gz: 4 (over z).
Axes of the slice: x: 2, y: 2, z: 4, core: 2. Of those that a mesh axis runs over, the one named last changes fastest.
Arguments:
- links: float32 [4, 3, 3, 2, 32, 16, 128], P(None, None, None, None, ('stream', 'ta'), 'gz'), parts along dimension 4, may hold values from -2.1 to 2.1
- force_in: float32 [4, 3, 3, 2, 32, 16, 128], P(None, None, None, None, ('stream', 'ta'), 'gz'), parts along dimension 4, may hold values from -6 to 6
Outputs:
- force_out: float32 [4, 3, 3, 2, 32, 16, 128], P(None, None, None, None, ('stream', 'ta'), 'gz'), parts along dimension 4
The draws below stay inside these ranges and needn't reach their ends.
There are 2 independent parts, one for each index of `stream`. The reference program is written for one: setup_inputs(seed, part) draws one part's arguments, and reference() takes and returns one part's arrays. A program takes and returns all parts, laid end to end along the dimension named above; each array names one. Nothing has to cross between parts.
All inputs are finite; a program needn't handle non-finite values.
Results may differ from the reference program's by a relative error of at most 0.0003.
Values sent between devices are 32-bit elements; how exact they have to be, the bound alone decides.
A program may use at most 128 MiB of HBM per device.

```python
import jax
import jax.numpy as jnp
from jax import lax

NY = 8
NX = 16
ORDER = 6
NT = 16
NZ = 16
YX = 128


def block_levels(key, shape, split, low, high):
    def one(dim, blocks):
        steps = jax.random.uniform(jax.random.fold_in(jax.random.fold_in(key, 6), dim), (blocks,), jnp.float32, low / len(split), high / len(split))
        return jnp.repeat(jnp.exp(steps), shape[dim] // blocks).reshape((-1,) + (1,) * (len(shape) - dim - 1))

    factor_of = one(*split[0])
    for cut in split[1:]:
        factor_of = factor_of * one(*cut)
    return factor_of


def normal_values(key, extent, spread, most, cuts=(), held_as=jnp.bfloat16):
    drawn = jax.random.normal(key, extent, jnp.float32) * spread
    if len(cuts) > 0:
        drawn = block_levels(key, extent, cuts, -0.22, 0.18) * drawn
    return jnp.clip(drawn, min=-most, max=most).astype(held_as)


def setup_inputs(seed: int = 0, part: int = 0) -> dict:
    key_of = jax.random.split(jax.random.key(seed), 3)
    own_keys = jax.random.split(jax.random.fold_in(key_of[2], part), 3)
    return {
        "links": normal_values(own_keys[0], (4, 3, 3, 2, NT, NZ, YX), 0.7, 2.1, ((4, 4), (5, 4)), jnp.float32),
        "force_in": normal_values(own_keys[1], (4, 3, 3, 2, NT, NZ, YX), 1.0, 6.0, ((4, 4), (5, 4)), jnp.float32),
    }


rho_value = 0.1

def product(left, right):
    left_real, left_imag = (left[:, :, 0], left[:, :, 1])
    right_real, right_imag = (right[:, :, 0], right[:, :, 1])
    real_part = lax.optimization_barrier(jnp.sum(left_real[:, :, None] * right_real[None] - left_imag[:, :, None] * right_imag[None], axis=1))
    imag_part = lax.optimization_barrier(jnp.sum(left_real[:, :, None] * right_imag[None] + left_imag[:, :, None] * right_real[None], axis=1))
    return jnp.stack([real_part, imag_part], axis=2)

def dagger(matrix):
    return jnp.stack([jnp.swapaxes(matrix[:, :, 0], 0, 1), -jnp.swapaxes(matrix[:, :, 1], 0, 1)], axis=2)

def offset_of(direction, orient):
    return tuple((orient if position == direction else 0 for position in range(4)))

def joined(first, second):
    return tuple((left_part + right_part for left_part, right_part in zip(first, second)))

def fat_link(links, direction, locate):
    anchor = (0, 0, 0, 0)
    center = locate(links[direction], anchor)
    ahead = offset_of(direction, 1)
    staple_sum = jnp.zeros_like(center)
    for other in range(4):
        if other == direction:
            continue
        beside = offset_of(other, 1)
        behind = offset_of(other, -1)
        upper_staple = product(product(locate(links[other], anchor), locate(links[direction], beside)), dagger(locate(links[other], ahead)))
        lower_staple = product(product(dagger(locate(links[other], behind)), locate(links[direction], behind)), locate(links[other], joined(ahead, behind)))
        staple_sum = staple_sum + upper_staple + lower_staple
    omega_field = product(rho_value * staple_sum, dagger(center))
    skew_part = 0.5 * (omega_field - dagger(omega_field))
    trace_part = skew_part[0, 0] + skew_part[1, 1] + skew_part[2, 2]
    trailing = (1,) * (center.ndim - 3)
    unit_three = jnp.eye(3, dtype=jnp.float32).reshape((3, 3, 1) + trailing)
    identity_field = unit_three * jnp.array([1.0, 0.0], jnp.float32).reshape((1, 1, 2) + trailing)
    generator = skew_part - unit_three * trace_part[None, None] / 3.0
    exponent = identity_field + generator / ORDER
    for degree in range(ORDER - 1, 0, -1):
        exponent = identity_field + product(generator, exponent) / degree
    return product(exponent, center)

def shifted(field, offset):
    moved = jnp.roll(field, (-offset[0], -offset[1]), axis=(3, 4))
    moved = jnp.roll(moved, -offset[2] * NX, axis=5)
    if offset[3] != 0:
        shape = moved.shape
        moved = jnp.roll(moved.reshape(shape[:5] + (NY, NX)), -offset[3], axis=6).reshape(shape)
    return moved

def reference(links, force_in):
    gradient = jnp.zeros_like(links)
    for direction in range(4):
        pull_back = jax.vjp(lambda whole: fat_link(whole, direction, shifted), links)[1]
        gradient = gradient + pull_back(force_in[direction])[0]
    return gradient
```

```python
import jax
import jax.numpy as jnp
from jax import lax
from jax.experimental import pallas as pl
from jax.experimental.pallas import tpu as pltpu
from jax.sharding import PartitionSpec as P

NX = 16
RHO = 0.1
MESH = pl.DeviceIdType.MESH
ROWS = 16
COMPS = 18
FLAT = ROWS * COMPS
CHUNK = 48
FACE = FLAT // 4
T_FIELDS = (1, 2, 3)
Z_FIELDS = (0, 2, 3)


def comp_rows(i, j, part, start):
    return pl.ds(pl.multiple_of(((i * 3 + j) * 2 + part) * ROWS + start, 8), 8)


def read(ref, index, start):
    return [
        [
            (ref[index, comp_rows(i, j, 0, start), :], ref[index, comp_rows(i, j, 1, start), :])
            for j in range(3)
        ]
        for i in range(3)
    ]


def write(ref, index, start, i, j, value):
    ref[index, comp_rows(i, j, 0, start), :] = value[0]
    ref[index, comp_rows(i, j, 1, start), :] = value[1]


def add_to(ref, index, start, i, j, value):
    ref[index, comp_rows(i, j, 0, start), :] += value[0]
    ref[index, comp_rows(i, j, 1, start), :] += value[1]


def entry(terms, i, j):
    real = imag = None
    real_less = imag_less = None
    for left, left_dag, right, right_dag in terms:
        for k in range(3):
            a = left[k][i] if left_dag else left[i][k]
            b = right[j][k] if right_dag else right[k][j]
            rr, ii, ri, ir = a[0] * b[0], a[1] * b[1], a[0] * b[1], a[1] * b[0]
            real = rr if real is None else real + rr
            if left_dag == right_dag:
                real_less = ii if real_less is None else real_less + ii
            else:
                real = real + ii
            if right_dag:
                imag_less = ri if imag_less is None else imag_less + ri
            else:
                imag = ri if imag is None else imag + ri
            if left_dag:
                imag_less = ir if imag_less is None else imag_less + ir
            else:
                imag = ir if imag is None else imag + ir
    if real_less is not None:
        real = real - real_less
    if imag_less is not None:
        imag = imag - imag_less
    return real, imag


def products(terms, emit):
    for i in range(3):
        for j in range(3):
            emit(i, j, entry(terms, i, j))


def matrix(terms):
    return [[entry(terms, i, j) for j in range(3)] for i in range(3)]


def cmul(a, b):
    return a[0] * b[0] - a[1] * b[1], a[0] * b[1] + a[1] * b[0]


def plane_of(p):
    first, second = p // 3, p // 5
    return first + second, p + 1 - 2 * first - second


def forward_plane(p, start, u, sh, c, d, pr):
    mu, nu = plane_of(p)
    beside, above = mu * 4 + nu, nu * 4 + mu
    left = lambda: read(u, mu, start)
    up = lambda: read(u, nu, start)
    b_ = lambda: read(sh, beside, start)
    c_ = lambda: read(sh, above, start)
    products([(left(), False, b_(), False)], lambda i, j, v: write(pr, 2 * p, start, i, j, v))
    products([(up(), False, c_(), False)], lambda i, j, v: write(pr, 2 * p + 1, start, i, j, v))
    pp = lambda: read(pr, 2 * p, start)
    rr = lambda: read(pr, 2 * p + 1, start)
    products([(rr(), False, b_(), True)], lambda i, j, v: add_to(c, mu, start, i, j, v))
    products([(up(), True, pp(), False)], lambda i, j, v: write(d, above, start, i, j, v))
    products([(pp(), False, c_(), True)], lambda i, j, v: add_to(c, nu, start, i, j, v))
    products([(left(), True, rr(), False)], lambda i, j, v: write(d, beside, start, i, j, v))


def backward_plane(p, start, u, sh, g, shg, out, d, pr, tmp):
    mu, nu = plane_of(p)
    beside, above = mu * 4 + nu, nu * 4 + mu
    a_ = lambda: read(u, mu, start)
    d_ = lambda: read(u, nu, start)
    b_ = lambda: read(sh, beside, start)
    c_ = lambda: read(sh, above, start)
    ga = lambda: read(g, mu, start)
    gd = lambda: read(g, nu, start)
    gb = lambda: read(shg, beside, start)
    gc = lambda: read(shg, above, start)
    pp = lambda: read(pr, 2 * p, start)
    rr = lambda: read(pr, 2 * p + 1, start)
    gp = lambda: read(tmp, 0, 0)
    gr = lambda: read(tmp, 1, 0)
    products(
        [(d_(), False, gc(), False), (gd(), False, c_(), False)],
        lambda i, j, v: write(tmp, 0, 0, i, j, v),
    )
    products(
        [(ga(), False, b_(), False), (a_(), False, gb(), False)],
        lambda i, j, v: write(tmp, 1, 0, i, j, v),
    )
    products(
        [(gp(), False, b_(), True), (rr(), False, gb(), True)],
        lambda i, j, v: add_to(out, mu, start, i, j, v),
    )
    products(
        [(a_(), True, gp(), False), (ga(), True, rr(), False)],
        lambda i, j, v: write(d, beside, start, i, j, v),
    )
    products(
        [(d_(), True, gr(), False), (gd(), True, pp(), False)],
        lambda i, j, v: write(d, above, start, i, j, v),
    )
    products(
        [(gr(), False, c_(), True), (pp(), False, gc(), True)],
        lambda i, j, v: add_to(out, nu, start, i, j, v),
    )


def hermitian(m):
    out = [[None] * 3 for _ in range(3)]
    for i in range(3):
        out[i][i] = (m[i][i][0], None)
        for j in range(i + 1, 3):
            re = 0.5 * (m[i][j][0] + m[j][i][0])
            im = 0.5 * (m[i][j][1] - m[j][i][1])
            out[i][j] = (re, im)
            out[j][i] = (re, -im)
    return out


def traceless(m):
    third = (m[0][0][0] + m[1][1][0] + m[2][2][0]) * (1.0 / 3.0)
    return [
        [(m[i][j][0] - third, None) if i == j else m[i][j] for j in range(3)] for i in range(3)
    ]


def times_h(a, b):
    if a[1] is None and b[1] is None:
        return a[0] * b[0], None
    if a[1] is None:
        return a[0] * b[0], a[0] * b[1]
    if b[1] is None:
        return a[0] * b[0], a[1] * b[0]
    return cmul(a, b)


def plus_h(a, b):
    if a is None:
        return b
    im = b[1] if a[1] is None else (a[1] if b[1] is None else a[1] + b[1])
    return a[0] + b[0], im


def entry_h(left, right, i, j):
    total = None
    for k in range(3):
        total = plus_h(total, times_h(left[i][k], right[k][j]))
    return total


def exponent_step(mu, start, u, c, f, g, out):
    link = read(u, mu, start)
    force = read(f, mu, start)
    grad_e = matrix([(force, False, link, True)])
    stap = read(c, mu, start)
    omega = matrix([(stap, False, link, True)])
    turned = [[(RHO * omega[i][j][1], -RHO * omega[i][j][0]) for j in range(3)] for i in range(3)]
    q = traceless(hermitian(turned))
    q2 = [[None] * 3 for _ in range(3)]
    for i in range(3):
        for j in range(i, 3):
            if i == j:
                total = q[i][i][0] * q[i][i][0]
                for k in range(3):
                    if k != i:
                        total = total + q[i][k][0] * q[i][k][0] + q[i][k][1] * q[i][k][1]
                q2[i][i] = (total, None)
            else:
                q2[i][j] = entry_h(q, q, i, j)
                q2[j][i] = (q2[i][j][0], -q2[i][j][1])
    c1 = 0.5 * (q2[0][0][0] + q2[1][1][0] + q2[2][2][0])
    n01 = q[0][1][0] * q[0][1][0] + q[0][1][1] * q[0][1][1]
    n02 = q[0][2][0] * q[0][2][0] + q[0][2][1] * q[0][2][1]
    n12 = q[1][2][0] * q[1][2][0] + q[1][2][1] * q[1][2][1]
    loop = cmul(q[0][1], q[1][2])
    c0 = (
        q[0][0][0] * (q[1][1][0] * q[2][2][0] - n12)
        - q[1][1][0] * n02
        - q[2][2][0] * n01
        + 2.0 * (loop[0] * q[0][2][0] + loop[1] * q[0][2][1])
    )
    f0 = (1.0 - c0 * c0 * (1.0 / 720), c0 * (c1 * (1.0 / 120) - 1.0 / 6))
    f1 = (c0 * (1.0 / 24 - c1 * (1.0 / 360)), 1.0 + c1 * (c1 * (1.0 / 120) - 1.0 / 6))
    f2 = (-0.5 + c1 * (1.0 / 24 - c1 * (1.0 / 720)), c0 * (1.0 / 120))
    expo = [[None] * 3 for _ in range(3)]
    for i in range(3):
        for j in range(3):
            value = plus_h(times_h(f1, q[i][j]), times_h(f2, q2[i][j]))
            if i == j:
                value = (value[0] + f0[0], value[1] + f0[1])
            expo[i][j] = value
    direct = matrix([(expo, True, force, False)])
    t0 = (
        grad_e[0][0][0] + grad_e[1][1][0] + grad_e[2][2][0],
        -(grad_e[0][0][1] + grad_e[1][1][1] + grad_e[2][2][1]),
    )

    def paired(h):
        re = im = None
        for i in range(3):
            for j in range(3):
                ge = grad_e[i][j]
                value = times_h((ge[0], -ge[1]), h[i][j])
                re = value[0] if re is None else re + value[0]
                im = value[1] if im is None else im + value[1]
        return re, im

    t1, t2 = paired(q), paired(q2)
    slope = 1.0 / 24 - c1 * (1.0 / 360)
    b0 = (
        t0[0] * (c0 * (-1.0 / 360))
        - t0[1] * (c1 * (1.0 / 120) - 1.0 / 6)
        + t1[0] * slope
        - t2[1] * (1.0 / 120)
    )
    b1 = (
        t2[0] * slope
        - t0[1] * (c0 * (1.0 / 120))
        - t1[0] * (c0 * (1.0 / 360))
        - t1[1] * (c1 * (1.0 / 60) - 1.0 / 6)
    )
    f1c, f2c = (f1[0], -f1[1]), (f2[0], -f2[1])
    first = hermitian([[cmul(f1c, grad_e[i][j]) for j in range(3)] for i in range(3)])
    second = hermitian([[cmul(f2c, grad_e[i][j]) for j in range(3)] for i in range(3)])
    mixed = [[entry_h(q, second, i, j) for j in range(3)] for i in range(3)]
    gq = [[None] * 3 for _ in range(3)]
    for i in range(3):
        gq[i][i] = (
            first[i][i][0] + 2.0 * mixed[i][i][0] + b1 * q[i][i][0] + b0 * q2[i][i][0],
            None,
        )
        for j in range(i + 1, 3):
            re = first[i][j][0] + mixed[i][j][0] + mixed[j][i][0]
            im = first[i][j][1] + mixed[i][j][1] - mixed[j][i][1]
            re = re + b1 * q[i][j][0] + b0 * q2[i][j][0]
            im = im + b1 * q[i][j][1] + b0 * q2[i][j][1]
            gq[i][j] = (re, im)
            gq[j][i] = (re, -im)
    gq = traceless(gq)
    gq = [
        [(RHO * e[0], None if e[1] is None else RHO * e[1]) for e in row] for row in gq
    ]
    for i in range(3):
        for j in range(3):
            re, im = entry_h(gq, link, i, j)
            write(g, mu, start, i, j, (-im, re))
    for i in range(3):
        for j in range(3):
            re, im = entry_h(gq, stap, i, j)
            write(out, mu, start, i, j, (direct[i][j][0] + im, direct[i][j][1] - re))


def chunks(body):
    def step(k, carry):
        body(pl.ds(pl.multiple_of(k * CHUNK, 8), CHUNK))
        return carry

    lax.fori_loop(0, FLAT // CHUNK, step, 0)


def lanes_x():
    return lax.broadcasted_iota(jnp.int32, (CHUNK, 128), 1) % NX


def row_number():
    return lax.broadcasted_iota(jnp.int32, (CHUNK, 128), 0) % ROWS


def shift_down_local(src, dst):
    def body(rows):
        last_x = lanes_x() == NX - 1
        for f in range(4):
            v = src[f, rows, :]
            if f != 0:
                dst[f, rows, :] = pltpu.roll(v, CHUNK - 4, 0)
            if f != 1:
                dst[4 + f, rows, :] = pltpu.roll(v, CHUNK - 1, 0)
            if f != 2:
                dst[8 + f, rows, :] = pltpu.roll(v, 128 - NX, 1)
            if f != 3:
                dst[12 + f, rows, :] = jnp.where(
                    last_x, pltpu.roll(v, NX - 1, 1), pltpu.roll(v, 127, 1)
                )

    chunks(body)


def shift_up_local(src, dst):
    def body(rows):
        first_x = lanes_x() == 0
        row = row_number()
        first_t = row < 4
        first_z = row % 4 == 0
        for f in range(4):
            total = dst[f, rows, :]
            if f != 0:
                total = total + jnp.where(first_t, 0.0, pltpu.roll(src[f, rows, :], 4, 0))
            if f != 1:
                total = total + jnp.where(first_z, 0.0, pltpu.roll(src[4 + f, rows, :], 1, 0))
            if f != 2:
                total = total + pltpu.roll(src[8 + f, rows, :], NX, 1)
            if f != 3:
                v = src[12 + f, rows, :]
                total = total + jnp.where(
                    first_x, pltpu.roll(v, 128 - NX + 1, 1), pltpu.roll(v, 1, 1)
                )
            dst[f, rows, :] = total

    chunks(body)


def pack_t(src, indices, row, buf, phase):
    for n, index in enumerate(indices):
        for c in range(COMPS):
            buf[phase, n, pl.ds(c * 4, 4), :] = src[index, pl.ds(c * ROWS + row, 4), :]


def pack_z(src, indices, row, buf, phase):
    for n, index in enumerate(indices):
        for k in range(FACE // 8):
            buf[phase, n, pl.ds(k * 8, 8), :] = src[index, pl.ds(k * 32 + row, 8, stride=4), :]


def put_t(dst, indices, row, buf, phase, add):
    for n, index in enumerate(indices):
        for c in range(COMPS):
            v = buf[phase, n, pl.ds(c * 4, 4), :]
            where = pl.ds(c * ROWS + row, 4)
            if add:
                v = v + dst[index, where, :]
            dst[index, where, :] = v


def put_z(dst, indices, row, buf, phase, add):
    for n, index in enumerate(indices):
        for k in range(FACE // 8):
            v = buf[phase, n, pl.ds(k * 8, 8), :]
            where = pl.ds(k * 32 + row, 8, stride=4)
            if add:
                v = v + dst[index, where, :]
            dst[index, where, :] = v


def make_kernel(n_t, n_z):
    def kernel(
        u, f, out, c, g, sh, shg, d, pr, tmp, t_out, t_in, z_out, z_in,
        t_send, t_recv, z_send, z_recv,
    ):
        me_t, me_z = lax.axis_index("ta"), lax.axis_index("gz")
        t_up, t_down = lax.rem(me_t + 1, n_t), lax.rem(me_t + n_t - 1, n_t)
        z_up, z_down = lax.rem(me_z + 1, n_z), lax.rem(me_z + n_z - 1, n_z)
        barrier = pltpu.get_barrier_semaphore()
        for target in ({"ta": t_up}, {"ta": t_down}, {"gz": z_up}, {"gz": z_down}):
            pl.semaphore_signal(barrier, inc=1, device_id=target, device_id_type=MESH)

        def copies(phase, to_t, to_z):
            return (
                pltpu.make_async_remote_copy(
                    src_ref=t_out.at[phase], dst_ref=t_in.at[phase],
                    send_sem=t_send.at[phase], recv_sem=t_recv.at[phase],
                    device_id={"ta": to_t}, device_id_type=MESH,
                ),
                pltpu.make_async_remote_copy(
                    src_ref=z_out.at[phase], dst_ref=z_in.at[phase],
                    send_sem=z_send.at[phase], recv_sem=z_recv.at[phase],
                    device_id={"gz": to_z}, device_id_type=MESH,
                ),
            )

        t_pairs = T_FIELDS
        z_pairs = tuple(4 + n for n in Z_FIELDS)

        def send(phase, to_t, to_z):
            pair = copies(phase, to_t, to_z)
            for copy in pair:
                copy.start()
            return pair

        def planes(low, high, body):
            def step(n, carry):
                body(n // 2, (n % 2) * 8)
                return carry

            lax.fori_loop(2 * low, 2 * high, step, 0)

        pack_t(u, T_FIELDS, 0, t_out, 0)
        pack_z(u, Z_FIELDS, 0, z_out, 0)
        pl.semaphore_wait(barrier, 4)
        pair = send(0, t_down, z_down)
        c[...] = jnp.zeros_like(c)
        shift_down_local(u, sh)
        run_forward = lambda p, start: forward_plane(p, start, u, sh, c, d, pr)
        planes(5, 6, run_forward)
        pair[0].wait()
        put_t(sh, t_pairs, 12, t_in, 0, False)
        pair[1].wait()
        put_z(sh, z_pairs, 3, z_in, 0, False)
        planes(0, 5, run_forward)
        pack_t(d, t_pairs, 12, t_out, 1)
        pack_z(d, z_pairs, 3, z_out, 1)
        pair = send(1, t_up, z_up)
        shift_up_local(d, c)
        pair[0].wait()
        put_t(c, T_FIELDS, 0, t_in, 1, True)
        pair[1].wait()
        put_z(c, Z_FIELDS, 0, z_in, 1, True)

        def expo(n, carry):
            exponent_step(n // 2, (n % 2) * 8, u, c, f, g, out)
            return carry

        lax.fori_loop(0, 8, expo, 0)
        pack_t(g, T_FIELDS, 0, t_out, 2)
        pack_z(g, Z_FIELDS, 0, z_out, 2)
        pair = send(2, t_down, z_down)
        shift_down_local(g, shg)
        run_backward = lambda p, start: backward_plane(
            p, start, u, sh, g, shg, out, d, pr, tmp
        )
        planes(5, 6, run_backward)
        pair[0].wait()
        put_t(shg, t_pairs, 12, t_in, 2, False)
        pair[1].wait()
        put_z(shg, z_pairs, 3, z_in, 2, False)
        planes(0, 5, run_backward)
        pack_t(d, t_pairs, 12, t_out, 3)
        pack_z(d, z_pairs, 3, z_out, 3)
        pair = send(3, t_up, z_up)
        shift_up_local(d, out)
        pair[0].wait()
        put_t(out, T_FIELDS, 0, t_in, 3, True)
        pair[1].wait()
        put_z(out, Z_FIELDS, 0, z_in, 3, True)

    return kernel


def per_device(links, force_in):
    kernel = make_kernel(lax.axis_size("ta"), lax.axis_size("gz"))
    fields = lambda n: pltpu.VMEM((n, FLAT, 128), jnp.float32)
    faces = pltpu.VMEM((4, 3, FACE, 128), jnp.float32)
    out = pl.pallas_call(
        kernel,
        out_shape=jax.ShapeDtypeStruct((4, FLAT, 128), jnp.float32),
        in_specs=[pl.BlockSpec(memory_space=pltpu.VMEM)] * 2,
        out_specs=pl.BlockSpec(memory_space=pltpu.VMEM),
        scratch_shapes=[
            fields(4), fields(4), fields(16), fields(16), fields(16), fields(12),
            pltpu.VMEM((2, FLAT, 128), jnp.float32),
            faces, faces, faces, faces,
            pltpu.SemaphoreType.DMA((4,)), pltpu.SemaphoreType.DMA((4,)),
            pltpu.SemaphoreType.DMA((4,)), pltpu.SemaphoreType.DMA((4,)),
        ],
        compiler_params=pltpu.CompilerParams(
            collective_id=0, has_side_effects=True, vmem_limit_bytes=32 * 1024 * 1024
        ),
    )(links.reshape(4, FLAT, 128), force_in.reshape(4, FLAT, 128))
    return out.reshape(links.shape)


def solution(mesh):
    placed = P(None, None, None, None, ("stream", "ta"), "gz", None)
    return jax.shard_map(
        per_device,
        mesh=mesh,
        in_specs=(placed, placed),
        out_specs=placed,
        check_vma=False,
    )
```

```python
import jax
import jax.numpy as jnp
from jax import lax
from jax.experimental import pallas as pl
from jax.experimental.pallas import tpu as pltpu
from jax.sharding import PartitionSpec as P

NX = 16
RHO = 0.1
MESH = pl.DeviceIdType.MESH
ROWS = 16
COMPS = 18
FLAT = ROWS * COMPS
CHUNK = 48
FACE = FLAT // 4
T_FIELDS = ((0, 1), (1, 2), (2, 3))
Z_FIELDS = ((0, 0), (1, 2), (2, 3))
ALL_FIELDS = ((0, 0), (1, 1), (2, 2), (3, 3))


def comp_rows(i, j, part, start):
    return pl.ds(pl.multiple_of(((i * 3 + j) * 2 + part) * ROWS + start, 8), 8)


def read(ref, index, start):
    return [
        [
            (ref[index, comp_rows(i, j, 0, start), :], ref[index, comp_rows(i, j, 1, start), :])
            for j in range(3)
        ]
        for i in range(3)
    ]


def write(ref, index, start, i, j, value):
    ref[index, comp_rows(i, j, 0, start), :] = value[0]
    ref[index, comp_rows(i, j, 1, start), :] = value[1]


def add_to(ref, index, start, i, j, value):
    ref[index, comp_rows(i, j, 0, start), :] += value[0]
    ref[index, comp_rows(i, j, 1, start), :] += value[1]


def entry(terms, i, j):
    real = imag = None
    real_less = imag_less = None
    for left, left_dag, right, right_dag in terms:
        for k in range(3):
            a = left[k][i] if left_dag else left[i][k]
            b = right[j][k] if right_dag else right[k][j]
            rr, ii, ri, ir = a[0] * b[0], a[1] * b[1], a[0] * b[1], a[1] * b[0]
            real = rr if real is None else real + rr
            if left_dag == right_dag:
                real_less = ii if real_less is None else real_less + ii
            else:
                real = real + ii
            if right_dag:
                imag_less = ri if imag_less is None else imag_less + ri
            else:
                imag = ri if imag is None else imag + ri
            if left_dag:
                imag_less = ir if imag_less is None else imag_less + ir
            else:
                imag = ir if imag is None else imag + ir
    if real_less is not None:
        real = real - real_less
    if imag_less is not None:
        imag = imag - imag_less
    return real, imag


def products(terms, emit):
    for i in range(3):
        for j in range(3):
            emit(i, j, entry(terms, i, j))


def matrix(terms):
    return [[entry(terms, i, j) for j in range(3)] for i in range(3)]


def cmul(a, b):
    return a[0] * b[0] - a[1] * b[1], a[0] * b[1] + a[1] * b[0]


def plane_of(p):
    first, second = p // 3, p // 5
    return first + second, p + 1 - 2 * first - second


def forward_plane(p, start, u, sh, c, d, pr):
    mu, nu = plane_of(p)
    beside, above = mu * 4 + nu, nu * 4 + mu
    left = lambda: read(u, mu, start)
    up = lambda: read(u, nu, start)
    b_ = lambda: read(sh, beside, start)
    c_ = lambda: read(sh, above, start)
    products([(left(), False, b_(), False)], lambda i, j, v: write(pr, 2 * p, start, i, j, v))
    products([(up(), False, c_(), False)], lambda i, j, v: write(pr, 2 * p + 1, start, i, j, v))
    pp = lambda: read(pr, 2 * p, start)
    rr = lambda: read(pr, 2 * p + 1, start)
    products([(rr(), False, b_(), True)], lambda i, j, v: add_to(c, mu, start, i, j, v))
    products([(up(), True, pp(), False)], lambda i, j, v: write(d, above, start, i, j, v))
    products([(pp(), False, c_(), True)], lambda i, j, v: add_to(c, nu, start, i, j, v))
    products([(left(), True, rr(), False)], lambda i, j, v: write(d, beside, start, i, j, v))


def backward_plane(p, start, u, sh, g, shg, out, d, pr, tmp):
    mu, nu = plane_of(p)
    beside, above = mu * 4 + nu, nu * 4 + mu
    a_ = lambda: read(u, mu, start)
    d_ = lambda: read(u, nu, start)
    b_ = lambda: read(sh, beside, start)
    c_ = lambda: read(sh, above, start)
    ga = lambda: read(g, mu, start)
    gd = lambda: read(g, nu, start)
    gb = lambda: read(shg, beside, start)
    gc = lambda: read(shg, above, start)
    pp = lambda: read(pr, 2 * p, start)
    rr = lambda: read(pr, 2 * p + 1, start)
    gp = lambda: read(tmp, 0, 0)
    gr = lambda: read(tmp, 1, 0)
    products(
        [(d_(), False, gc(), False), (gd(), False, c_(), False)],
        lambda i, j, v: write(tmp, 0, 0, i, j, v),
    )
    products(
        [(ga(), False, b_(), False), (a_(), False, gb(), False)],
        lambda i, j, v: write(tmp, 1, 0, i, j, v),
    )
    products(
        [(gp(), False, b_(), True), (rr(), False, gb(), True)],
        lambda i, j, v: add_to(out, mu, start, i, j, v),
    )
    products(
        [(a_(), True, gp(), False), (ga(), True, rr(), False)],
        lambda i, j, v: write(d, beside, start, i, j, v),
    )
    products(
        [(d_(), True, gr(), False), (gd(), True, pp(), False)],
        lambda i, j, v: write(d, above, start, i, j, v),
    )
    products(
        [(gr(), False, c_(), True), (pp(), False, gc(), True)],
        lambda i, j, v: add_to(out, nu, start, i, j, v),
    )


def hermitian(m):
    out = [[None] * 3 for _ in range(3)]
    for i in range(3):
        out[i][i] = (m[i][i][0], None)
        for j in range(i + 1, 3):
            re = 0.5 * (m[i][j][0] + m[j][i][0])
            im = 0.5 * (m[i][j][1] - m[j][i][1])
            out[i][j] = (re, im)
            out[j][i] = (re, -im)
    return out


def traceless(m):
    third = (m[0][0][0] + m[1][1][0] + m[2][2][0]) * (1.0 / 3.0)
    return [
        [(m[i][j][0] - third, None) if i == j else m[i][j] for j in range(3)] for i in range(3)
    ]


def times_h(a, b):
    if a[1] is None and b[1] is None:
        return a[0] * b[0], None
    if a[1] is None:
        return a[0] * b[0], a[0] * b[1]
    if b[1] is None:
        return a[0] * b[0], a[1] * b[0]
    return cmul(a, b)


def plus_h(a, b):
    if a is None:
        return b
    im = b[1] if a[1] is None else (a[1] if b[1] is None else a[1] + b[1])
    return a[0] + b[0], im


def entry_h(left, right, i, j):
    total = None
    for k in range(3):
        total = plus_h(total, times_h(left[i][k], right[k][j]))
    return total


def exponent_step(mu, start, u, c, f, g, out):
    link = read(u, mu, start)
    force = read(f, mu, start)
    grad_e = matrix([(force, False, link, True)])
    stap = read(c, mu, start)
    omega = matrix([(stap, False, link, True)])
    turned = [[(RHO * omega[i][j][1], -RHO * omega[i][j][0]) for j in range(3)] for i in range(3)]
    q = traceless(hermitian(turned))
    q2 = [[None] * 3 for _ in range(3)]
    for i in range(3):
        for j in range(i, 3):
            if i == j:
                total = q[i][i][0] * q[i][i][0]
                for k in range(3):
                    if k != i:
                        total = total + q[i][k][0] * q[i][k][0] + q[i][k][1] * q[i][k][1]
                q2[i][i] = (total, None)
            else:
                q2[i][j] = entry_h(q, q, i, j)
                q2[j][i] = (q2[i][j][0], -q2[i][j][1])
    c1 = 0.5 * (q2[0][0][0] + q2[1][1][0] + q2[2][2][0])
    n01 = q[0][1][0] * q[0][1][0] + q[0][1][1] * q[0][1][1]
    n02 = q[0][2][0] * q[0][2][0] + q[0][2][1] * q[0][2][1]
    n12 = q[1][2][0] * q[1][2][0] + q[1][2][1] * q[1][2][1]
    loop = cmul(q[0][1], q[1][2])
    c0 = (
        q[0][0][0] * (q[1][1][0] * q[2][2][0] - n12)
        - q[1][1][0] * n02
        - q[2][2][0] * n01
        + 2.0 * (loop[0] * q[0][2][0] + loop[1] * q[0][2][1])
    )
    f0 = (1.0 - c0 * c0 * (1.0 / 720), c0 * (c1 * (1.0 / 120) - 1.0 / 6))
    f1 = (c0 * (1.0 / 24 - c1 * (1.0 / 360)), 1.0 + c1 * (c1 * (1.0 / 120) - 1.0 / 6))
    f2 = (-0.5 + c1 * (1.0 / 24 - c1 * (1.0 / 720)), c0 * (1.0 / 120))
    expo = [[None] * 3 for _ in range(3)]
    for i in range(3):
        for j in range(3):
            value = plus_h(times_h(f1, q[i][j]), times_h(f2, q2[i][j]))
            if i == j:
                value = (value[0] + f0[0], value[1] + f0[1])
            expo[i][j] = value
    direct = matrix([(expo, True, force, False)])
    t0 = (
        grad_e[0][0][0] + grad_e[1][1][0] + grad_e[2][2][0],
        -(grad_e[0][0][1] + grad_e[1][1][1] + grad_e[2][2][1]),
    )

    def paired(h):
        re = im = None
        for i in range(3):
            for j in range(3):
                ge = grad_e[i][j]
                value = times_h((ge[0], -ge[1]), h[i][j])
                re = value[0] if re is None else re + value[0]
                im = value[1] if im is None else im + value[1]
        return re, im

    t1, t2 = paired(q), paired(q2)
    slope = 1.0 / 24 - c1 * (1.0 / 360)
    b0 = (
        t0[0] * (c0 * (-1.0 / 360))
        - t0[1] * (c1 * (1.0 / 120) - 1.0 / 6)
        + t1[0] * slope
        - t2[1] * (1.0 / 120)
    )
    b1 = (
        t2[0] * slope
        - t0[1] * (c0 * (1.0 / 120))
        - t1[0] * (c0 * (1.0 / 360))
        - t1[1] * (c1 * (1.0 / 60) - 1.0 / 6)
    )
    f1c, f2c = (f1[0], -f1[1]), (f2[0], -f2[1])
    first = hermitian([[cmul(f1c, grad_e[i][j]) for j in range(3)] for i in range(3)])
    second = hermitian([[cmul(f2c, grad_e[i][j]) for j in range(3)] for i in range(3)])
    mixed = [[entry_h(q, second, i, j) for j in range(3)] for i in range(3)]
    gq = [[None] * 3 for _ in range(3)]
    for i in range(3):
        gq[i][i] = (
            first[i][i][0] + 2.0 * mixed[i][i][0] + b1 * q[i][i][0] + b0 * q2[i][i][0],
            None,
        )
        for j in range(i + 1, 3):
            re = first[i][j][0] + mixed[i][j][0] + mixed[j][i][0]
            im = first[i][j][1] + mixed[i][j][1] - mixed[j][i][1]
            re = re + b1 * q[i][j][0] + b0 * q2[i][j][0]
            im = im + b1 * q[i][j][1] + b0 * q2[i][j][1]
            gq[i][j] = (re, im)
            gq[j][i] = (re, -im)
    gq = traceless(gq)
    gq = [
        [(RHO * e[0], None if e[1] is None else RHO * e[1]) for e in row] for row in gq
    ]
    for i in range(3):
        for j in range(3):
            re, im = entry_h(gq, link, i, j)
            write(g, mu, start, i, j, (-im, re))
    for i in range(3):
        for j in range(3):
            re, im = entry_h(gq, stap, i, j)
            write(out, mu, start, i, j, (direct[i][j][0] + im, direct[i][j][1] - re))


def chunks(body):
    def step(k, carry):
        body(pl.ds(pl.multiple_of(k * CHUNK, 8), CHUNK))
        return carry

    lax.fori_loop(0, FLAT // CHUNK, step, 0)


def lanes_x():
    return lax.broadcasted_iota(jnp.int32, (CHUNK, 128), 1) % NX


def row_number():
    return lax.broadcasted_iota(jnp.int32, (CHUNK, 128), 0) % ROWS


def shift_down_local(src, dst):
    def body(rows):
        last_x = lanes_x() == NX - 1
        for f in range(4):
            v = src[f, rows, :]
            if f != 0:
                dst[f, rows, :] = pltpu.roll(v, CHUNK - 4, 0)
            if f != 1:
                dst[4 + f, rows, :] = pltpu.roll(v, CHUNK - 1, 0)
            if f != 2:
                dst[8 + f, rows, :] = pltpu.roll(v, 128 - NX, 1)
            if f != 3:
                dst[12 + f, rows, :] = jnp.where(
                    last_x, pltpu.roll(v, NX - 1, 1), pltpu.roll(v, 127, 1)
                )

    chunks(body)


def shift_up_local(src, dst):
    def body(rows):
        first_x = lanes_x() == 0
        row = row_number()
        first_t = row < 4
        first_z = row % 4 == 0
        for f in range(4):
            total = dst[f, rows, :]
            if f != 0:
                total = total + jnp.where(first_t, 0.0, pltpu.roll(src[f, rows, :], 4, 0))
            if f != 1:
                total = total + jnp.where(first_z, 0.0, pltpu.roll(src[4 + f, rows, :], 1, 0))
            if f != 2:
                total = total + pltpu.roll(src[8 + f, rows, :], NX, 1)
            if f != 3:
                v = src[12 + f, rows, :]
                total = total + jnp.where(
                    first_x, pltpu.roll(v, 128 - NX + 1, 1), pltpu.roll(v, 1, 1)
                )
            dst[f, rows, :] = total

    chunks(body)


def pack_t(src, pairs, row, buf, phase):
    for n, index in pairs:
        for c in range(COMPS):
            buf[phase, n, pl.ds(c * 4, 4), :] = src[index, pl.ds(c * ROWS + row, 4), :]


def pack_z(src, pairs, row, buf, phase):
    for n, index in pairs:
        for k in range(FACE // 8):
            buf[phase, n, pl.ds(k * 8, 8), :] = src[index, pl.ds(k * 32 + row, 8, stride=4), :]


def put_t(dst, pairs, row, buf, phase, add):
    for n, index in pairs:
        for c in range(COMPS):
            v = buf[phase, n, pl.ds(c * 4, 4), :]
            where = pl.ds(c * ROWS + row, 4)
            if add:
                v = v + dst[index, where, :]
            dst[index, where, :] = v


def put_z(dst, pairs, row, buf, phase, add):
    for n, index in pairs:
        for k in range(FACE // 8):
            v = buf[phase, n, pl.ds(k * 8, 8), :]
            where = pl.ds(k * 32 + row, 8, stride=4)
            if add:
                v = v + dst[index, where, :]
            dst[index, where, :] = v


def pack_corner(src, buf, phase):
    for first, count in ((0, 8), (8, 8), (16, 2)):
        buf[phase, pl.ds(first, count), :] = src[
            1, pl.ds(first * ROWS + 3, count, stride=ROWS), :
        ]


def layer_beside(layer, phase, corner, dst, base):
    v = layer[phase, 1]
    lane = lax.broadcasted_iota(jnp.int32, v.shape, 1) % NX
    dst[base] = pltpu.roll(v, FACE - 1, 0)
    for first, count in ((0, 8), (8, 8), (16, 2)):
        dst[base, pl.ds(first * 4 + 3, count, stride=4), :] = corner[phase, pl.ds(first, count), :]
    dst[base + 1] = pltpu.roll(v, 128 - NX, 1)
    dst[base + 2] = jnp.where(lane == NX - 1, pltpu.roll(v, NX - 1, 1), pltpu.roll(v, 127, 1))


def read_layer(ref, *index):
    def part(c):
        return ref[(*index, pl.ds(c * 4, 4), slice(None))]

    return [
        [(part((i * 3 + j) * 2), part((i * 3 + j) * 2 + 1)) for j in range(3)] for i in range(3)
    ]


def layer_writer(ref, phase, n):
    def emit(i, j, value):
        c = (i * 3 + j) * 2
        ref[phase, n, pl.ds(c * 4, 4), :] = value[0]
        ref[phase, n, pl.ds(c * 4 + 4, 4), :] = value[1]

    return emit


def forward_layer(n, mu, layer, beside, result):
    low = read_layer(layer, 0, 1)
    pp = matrix([(read_layer(layer, 0, mu), False, read_layer(beside, n), False)])
    products([(low, True, pp, False)], layer_writer(result, 0, n))


def backward_layer(n, mu, layer, beside, result):
    a, b = read_layer(layer, 0, mu), read_layer(beside, n)
    ga, gb = read_layer(layer, 1, mu), read_layer(beside, 3 + n)
    gr = matrix([(ga, False, b, False), (a, False, gb, False)])
    pp = matrix([(a, False, b, False)])
    products(
        [(read_layer(layer, 0, 1), True, gr, False), (read_layer(layer, 1, 1), True, pp, False)],
        layer_writer(result, 1, n),
    )


def make_kernel(n_t, n_z):
    def kernel(
        u_hbm, f_hbm, out, u, f, c, g, sh, shg, d, pr, tmp, t_out, t_in, z_out, z_in,
        l_out, l_in, k_out, k_in, beside, local,
        t_send, t_recv, z_send, z_recv, l_send, l_recv, k_send, k_recv, load_sem,
    ):
        me_t, me_z = lax.axis_index("ta"), lax.axis_index("gz")
        t_up, t_down = lax.rem(me_t + 1, n_t), lax.rem(me_t + n_t - 1, n_t)
        z_up, z_down = lax.rem(me_z + 1, n_z), lax.rem(me_z + n_z - 1, n_z)
        loads = [pltpu.make_async_copy(u_hbm.at[k], u.at[k], load_sem.at[k]) for k in range(4)]
        loads += [
            pltpu.make_async_copy(f_hbm.at[k], f.at[k], load_sem.at[4 + k]) for k in range(4)
        ]
        for load in loads:
            load.start()
        barrier = pltpu.get_barrier_semaphore()
        for target in (
            {"ta": t_up}, {"ta": t_down}, {"gz": z_up}, {"gz": z_down},
            {"ta": t_down, "gz": z_up}, {"ta": t_up, "gz": z_down},
        ):
            pl.semaphore_signal(barrier, inc=1, device_id=target, device_id_type=MESH)

        t_pairs = T_FIELDS
        z_pairs = tuple((n, 4 + index) for n, index in Z_FIELDS)
        sent = []

        def send(out_buf, in_buf, send_sem, recv_sem, slot, place, target):
            copy = pltpu.make_async_remote_copy(
                src_ref=out_buf.at[slot], dst_ref=in_buf.at[slot],
                send_sem=send_sem.at[place], recv_sem=recv_sem.at[place],
                device_id=target, device_id_type=MESH,
            )
            copy.start()
            sent.append(copy)
            return copy

        def send_t(phase, n, target):
            return send(t_out, t_in, t_send, t_recv, (phase, n), phase * 3 + n, {"ta": target})

        def send_z(phase, n):
            return send(z_out, z_in, z_send, z_recv, (phase, n), phase * 3 + n, {"gz": z_down})

        def send_layer(phase, n):
            return send(l_out, l_in, l_send, l_recv, (phase, n), phase * 4 + n, {"gz": z_up})

        def send_corner(phase):
            target = {"ta": t_down, "gz": z_up}
            return send(k_out, k_in, k_send, k_recv, phase, phase, target)

        def finish(copies):
            for copy in copies:
                copy.wait_recv()

        def planes(low, high, body):
            def step(n, carry):
                body(n // 2, (n % 2) * 8)
                return carry

            lax.fori_loop(2 * low, 2 * high, step, 0)

        for load in loads[:4]:
            load.wait()
        pack_z(u, Z_FIELDS, 0, z_out, 0)
        pack_corner(u, k_out, 0)
        pl.semaphore_wait(barrier, 6)
        z_copies = [send_z(0, n) for n in range(3)]
        k_copy = send_corner(0)
        pack_t(u, T_FIELDS, 0, t_out, 0)
        t_copies = [send_t(0, n, t_down) for n in range(3)]
        pack_z(u, ALL_FIELDS, 3, l_out, 0)
        l_copies = [send_layer(0, n) for n in range(4)]
        c[...] = jnp.zeros_like(c)
        shift_down_local(u, sh)
        run_forward = lambda p, start: forward_plane(p, start, u, sh, c, d, pr)
        planes(5, 6, run_forward)
        finish(t_copies)
        put_t(sh, t_pairs, 12, t_in, 0, False)
        planes(1, 3, run_forward)
        pack_t(d, t_pairs[1:], 12, t_out, 1)
        t_copies = [send_t(1, n, t_up) for n in (1, 2)]
        finish(z_copies)
        put_z(sh, z_pairs, 3, z_in, 0, False)
        planes(0, 1, run_forward)
        pack_t(d, t_pairs[:1], 12, t_out, 1)
        t_copies.append(send_t(1, 0, t_up))
        planes(3, 5, run_forward)
        shift_up_local(d, c)
        finish(l_copies)
        k_copy.wait_recv()
        layer_beside(l_in, 0, k_in, beside, 0)
        for n, mu in Z_FIELDS:
            forward_layer(n, mu, l_in, beside, local)
        put_z(c, Z_FIELDS, 0, local, 0, True)
        finish(t_copies)
        put_t(c, T_FIELDS, 0, t_in, 1, True)

        for load in loads[4:]:
            load.wait()
        z_copies, t_copies, l_copies = [], [], []
        for mu in (1, 0, 2, 3):

            def expo(n, carry, mu=mu):
                exponent_step(mu, n * 8, u, c, f, g, out)
                return carry

            lax.fori_loop(0, 2, expo, 0)
            pack_z(g, ALL_FIELDS[mu : mu + 1], 3, l_out, 1)
            l_copies.append(send_layer(1, mu))
            if mu == 1:
                pack_corner(g, k_out, 1)
                k_copy = send_corner(1)
            else:
                n = (0, 1, 1, 2)[mu]
                pack_z(g, ((n, mu),), 0, z_out, 1)
                z_copies.append(send_z(1, n))
            if mu != 0:
                pack_t(g, ((mu - 1, mu),), 0, t_out, 2)
                t_copies.append(send_t(2, mu - 1, t_down))
        shift_down_local(g, shg)
        run_backward = lambda p, start: backward_plane(
            p, start, u, sh, g, shg, out, d, pr, tmp
        )
        planes(5, 6, run_backward)
        finish(t_copies)
        put_t(shg, t_pairs, 12, t_in, 2, False)
        planes(1, 3, run_backward)
        pack_t(d, t_pairs[1:], 12, t_out, 3)
        t_copies = [send_t(3, n, t_up) for n in (1, 2)]
        finish(z_copies)
        put_z(shg, z_pairs, 3, z_in, 1, False)
        planes(0, 1, run_backward)
        pack_t(d, t_pairs[:1], 12, t_out, 3)
        t_copies.append(send_t(3, 0, t_up))
        planes(3, 5, run_backward)
        shift_up_local(d, out)
        finish(l_copies)
        k_copy.wait_recv()
        layer_beside(l_in, 1, k_in, beside, 3)
        for n, mu in Z_FIELDS:
            backward_layer(n, mu, l_in, beside, local)
        put_z(out, Z_FIELDS, 0, local, 1, True)
        finish(t_copies)
        put_t(out, T_FIELDS, 0, t_in, 3, True)
        for copy in sent:
            copy.wait_send()

    return kernel


def per_device(links, force_in):
    kernel = make_kernel(lax.axis_size("ta"), lax.axis_size("gz"))
    held = lambda *extent: pltpu.VMEM((*extent, 128), jnp.float32)
    fields = lambda n: held(n, FLAT)
    sems = lambda n: pltpu.SemaphoreType.DMA((n,))
    out = pl.pallas_call(
        kernel,
        out_shape=jax.ShapeDtypeStruct((4, FLAT, 128), jnp.float32),
        in_specs=[pl.BlockSpec(memory_space=pltpu.HBM)] * 2,
        out_specs=pl.BlockSpec(memory_space=pltpu.VMEM),
        scratch_shapes=[
            fields(4), fields(4),
            fields(4), fields(4), fields(16), fields(16), fields(16), fields(12), fields(2),
            held(4, 3, FACE), held(4, 3, FACE), held(2, 3, FACE), held(2, 3, FACE),
            held(2, 4, FACE), held(2, 4, FACE), held(2, 24), held(2, 24),
            held(6, FACE), held(2, 3, FACE),
            sems(12), sems(12), sems(6), sems(6), sems(8), sems(8), sems(2), sems(2), sems(8),
        ],
        compiler_params=pltpu.CompilerParams(
            collective_id=0, has_side_effects=True, vmem_limit_bytes=32 * 1024 * 1024
        ),
    )(links.reshape(4, FLAT, 128), force_in.reshape(4, FLAT, 128))
    return out.reshape(links.shape)


def solution(mesh):
    placed = P(None, None, None, None, ("stream", "ta"), "gz", None)
    return jax.shard_map(
        per_device,
        mesh=mesh,
        in_specs=(placed, placed),
        out_specs=placed,
        check_vma=False,
    )
```
